32 devices in a mesh: band: 4 (over y, x), pix: 8 (over z, core).
Axes of the slice: x: 2, y: 2, z: 4, core: 2. Of those that a mesh axis runs over, the one named last changes fastest.
Arguments:
- pixels: bfloat16 [128, 8, 1024], P('pix', 'band'), may hold values from -6 to 6
- clear_count: int32 [8], P('pix'), may hold values from 3 to 10, as said below
- clear_index: int32 [80], P('pix'), may hold values from 0 to 15, as said below
- attn_gain: float32 [1024], replicated, may hold values from 0.1 to 1.9
- w_query: bfloat16 [1024, 1024], P(None, 'band')
- w_key: bfloat16 [1024, 1024], P(None, 'band')
- w_value: bfloat16 [1024, 1024], P(None, 'band'), may hold values from -0.1875 to 0.1875
- w_out: bfloat16 [1024, 1024], P('band'), may hold values from -0.1875 to 0.1875
- mlp_gain: float32 [1024], replicated, may hold values from 0.1 to 1.9
- w_gate: bfloat16 [1024, 4096], P(None, 'band'), may hold values from -0.1875 to 0.1875
- w_up: bfloat16 [1024, 4096], P(None, 'band'), may hold values from -0.1875 to 0.1875
- w_down: bfloat16 [4096, 1024], P('band'), may hold values from -0.09375 to 0.09375
Outputs:
- updated: bfloat16 [128, 8, 1024], P('pix', 'band')
The draws below stay inside these ranges and needn't reach their ends.
Inputs may be any that keep to these rules, and one draw needn't show every extreme that they name: `clear_count`: some tile, drawn from the seed, keeps exactly 10 clear pixels. `clear_index`: for tile t, entries t*10 to t*10+clear_count[t]-1 are distinct local pixel indices in rising order; the tile's remaining entries are 0.
All inputs are finite; a program needn't handle non-finite values.
Results may differ from the reference program's by a relative error of at most 0.019.
Values may be sent and summed in bfloat16 or wider, within the bound.
A program may use at most 64 MiB of HBM per device.

```python
import jax
import jax.numpy as jnp
from jax import lax

D = 1024
HEADS = 16
HD = 64
FF = 4096
PIX_DEV = 16
CAP = 10
MIN_KEEP = 3
SPEC = 8
PIXELS = 128
N_BAND = 4
N_PIX = 8


def coupled_pair(key):
    base = jax.random.normal(jax.random.fold_in(key, 11), (D, HEADS * HD), jnp.float32) * D ** (-0.5)
    other = jax.random.normal(jax.random.fold_in(key, 12), (D, HEADS * HD), jnp.float32) * D ** (-0.5)
    return (1.7 * base, 1.7 * other)


def draw_w_query(key, part):
    return coupled_pair(key)[0].astype(jnp.bfloat16)


def draw_w_key(key, part):
    return coupled_pair(key)[1].astype(jnp.bfloat16)


def clear_lists(key):
    counts = jax.random.randint(jax.random.fold_in(key, 21), (N_PIX,), MIN_KEEP, CAP + 1)
    full_tile = jax.random.randint(jax.random.fold_in(key, 22), (), 0, N_PIX)
    counts = jnp.where(jnp.arange(N_PIX) == full_tile, CAP, counts)
    scores = jax.random.randint(jax.random.fold_in(key, 23), (N_PIX, PIX_DEV), 0, 1 << 20)
    scores = scores * PIX_DEV + jnp.arange(PIX_DEV)[None, :]
    ranks = jnp.argsort(jnp.argsort(scores, axis=1), axis=1)
    chosen = ranks < counts[:, None]
    positions = jnp.arange(PIX_DEV)[None, :]
    order = jnp.where(chosen, positions, PIX_DEV + positions)
    picked = jnp.argsort(order, axis=1)[:, :CAP]
    picked = jnp.where(jnp.arange(CAP)[None, :] < counts[:, None], picked, 0)
    return (counts.astype(jnp.int32), picked.reshape(N_PIX * CAP).astype(jnp.int32))


def draw_clear_count(key, part):
    return clear_lists(key)[0]


def draw_clear_index(key, part):
    return clear_lists(key)[1]


def level_of(key, extent, pieces, low, high):
    factor_of, own = 1.0, jax.random.fold_in(key, 6)
    for position, parts in pieces:
        steps = jnp.exp(jax.random.uniform(jax.random.fold_in(own, position), (parts,), jnp.float32, low / len(pieces), high / len(pieces)))
        factor_of = factor_of * jnp.repeat(steps, extent[position] // parts).reshape([-1 if axis == position else 1 for axis in range(len(extent))])
    return factor_of


def gaussian(key, extent, deviation, reach, pieces=(), kind=jnp.bfloat16):
    factor_of = level_of(key, extent, pieces, -0.22, 0.18) if pieces else 1.0
    entries = jax.random.normal(key, extent, jnp.float32) * deviation * factor_of
    return jnp.minimum(jnp.maximum(entries, -reach), reach).astype(kind)


def setup_inputs(seed: int = 0) -> dict:
    seeds = jax.random.split(jax.random.key(seed), 13)
    pixels = gaussian(seeds[0], (PIXELS, SPEC, D), 1.0, 6.0, ((0, 8), (1, 4)))
    clear_count = draw_clear_count(jax.random.fold_in(seeds[12], 71), 0)
    clear_index = draw_clear_index(jax.random.fold_in(seeds[12], 71), 0)
    attn_gain = jnp.clip(1.0 + 0.18 * jax.random.normal(seeds[3], (D,), jnp.float32), 0.1, 1.9)
    w_query = draw_w_query(jax.random.fold_in(seeds[12], 71), 0)
    w_key = draw_w_key(jax.random.fold_in(seeds[12], 71), 0)
    w_value = gaussian(seeds[6], (D, HEADS * HD), D ** -0.5, 0.1875, ((1, 4),))
    w_out = gaussian(seeds[7], (HEADS * HD, D), (HEADS * HD) ** -0.5, 0.1875, ((0, 4),))
    mlp_gain = jnp.clip(1.0 + 0.18 * jax.random.normal(seeds[8], (D,), jnp.float32), 0.1, 1.9)
    w_gate = gaussian(seeds[9], (D, FF), D ** -0.5, 0.1875, ((1, 4),))
    w_up = gaussian(seeds[10], (D, FF), D ** -0.5, 0.1875, ((1, 4),))
    w_down = gaussian(seeds[11], (FF, D), FF ** -0.5, 0.09375, ((0, 4),))
    return {"pixels": pixels, "clear_count": clear_count, "clear_index": clear_index, "attn_gain": attn_gain, "w_query": w_query, "w_key": w_key, "w_value": w_value, "w_out": w_out, "mlp_gain": mlp_gain, "w_gate": w_gate, "w_up": w_up, "w_down": w_down}


def normed(rows, gain):
    full = rows.astype(jnp.float32)
    scaled = full * lax.rsqrt(lax.optimization_barrier(jnp.mean(full * full, axis=-1, keepdims=True)) + 1e-05)
    return (scaled * gain.astype(jnp.float32)).astype(jnp.bfloat16)

def reference(pixels, clear_count, clear_index, attn_gain, w_query, w_key, w_value, w_out, mlp_gain, w_gate, w_up, w_down):
    tiles = pixels.reshape(N_PIX, PIX_DEV, SPEC, D)
    slots = clear_index.reshape(N_PIX, CAP).astype(jnp.int32)
    kept = jnp.take_along_axis(tiles, slots[:, :, None, None], axis=1)
    rows = jnp.transpose(kept, (2, 0, 1, 3)).reshape(SPEC, N_PIX * CAP, D)
    live_slot = jnp.arange(CAP, dtype=jnp.int32)[None, :] < clear_count[:, None]
    live = live_slot.reshape(N_PIX * CAP)
    flat = normed(rows, attn_gain).reshape(SPEC * N_PIX * CAP, D)

    def project(weight):
        out = jnp.dot(flat, weight, preferred_element_type=jnp.float32).astype(jnp.bfloat16)
        return out.reshape(SPEC, N_PIX * CAP, HEADS, HD)
    query = project(w_query)
    key = project(w_key)
    value = project(w_value)

    def attend(block):
        q_rows, k_rows, v_rows = block
        scores = jnp.einsum('qhd,khd->hqk', q_rows.astype(jnp.float32), k_rows.astype(jnp.float32)) * HD ** (-0.5)
        masked = jnp.where(live[None, None, :], scores, -1e+30)
        top = lax.optimization_barrier(jnp.max(masked, axis=-1, keepdims=True))
        expo = jnp.where(live[None, None, :], jnp.exp(masked - top), 0.0)
        totals = lax.optimization_barrier(jnp.sum(expo, axis=-1))
        weights = expo.astype(jnp.bfloat16)
        mixed = jnp.einsum('hqk,khd->qhd', weights.astype(jnp.float32), v_rows.astype(jnp.float32))
        return (mixed / jnp.transpose(totals)[:, :, None]).astype(jnp.bfloat16)
    context = lax.map(attend, (query, key, value))
    context_groups = context.reshape(SPEC * N_PIX * CAP, N_BAND, HEADS * HD // N_BAND)
    out_groups = w_out.reshape(N_BAND, HEADS * HD // N_BAND, D)

    def add_attn(total, group):
        piece = lax.dynamic_index_in_dim(context_groups, group, 1, keepdims=False)
        weight = lax.dynamic_index_in_dim(out_groups, group, 0, keepdims=False)
        part = jnp.dot(piece, weight, preferred_element_type=jnp.float32).astype(jnp.bfloat16)
        part = lax.optimization_barrier(part)
        return (total + part.astype(jnp.float32), None)
    groups = jnp.arange(N_BAND, dtype=jnp.int32)
    attn_out, _ = lax.scan(add_attn, jnp.zeros((SPEC * N_PIX * CAP, D), jnp.float32), groups)
    state = (rows.reshape(SPEC * N_PIX * CAP, D).astype(jnp.float32) + attn_out).astype(jnp.bfloat16)
    mlp_in = normed(state, mlp_gain)
    gate_groups = w_gate.reshape(D, N_BAND, FF // N_BAND)
    up_groups = w_up.reshape(D, N_BAND, FF // N_BAND)
    down_groups = w_down.reshape(N_BAND, FF // N_BAND, D)

    def add_mlp(total, group):
        gate = jnp.dot(mlp_in, lax.dynamic_index_in_dim(gate_groups, group, 1, keepdims=False), preferred_element_type=jnp.float32)
        upper = jnp.dot(mlp_in, lax.dynamic_index_in_dim(up_groups, group, 1, keepdims=False), preferred_element_type=jnp.float32)
        hidden = (jax.nn.silu(gate) * upper).astype(jnp.bfloat16)
        part = jnp.dot(hidden, lax.dynamic_index_in_dim(down_groups, group, 0, keepdims=False), preferred_element_type=jnp.float32).astype(jnp.bfloat16)
        part = lax.optimization_barrier(part)
        return (total + part.astype(jnp.float32), None)
    mlp_out, _ = lax.scan(add_mlp, jnp.zeros((SPEC * N_PIX * CAP, D), jnp.float32), groups)
    encoded = (state.astype(jnp.float32) + mlp_out).astype(jnp.bfloat16)
    result = jnp.transpose(encoded.reshape(SPEC, N_PIX, CAP, D), (1, 2, 0, 3))
    chosen = (jnp.arange(PIX_DEV, dtype=jnp.int32)[None, :, None] == slots[:, None, :]) & live_slot[:, None, :]
    placed = jnp.einsum('tpc,tcsd->tpsd', chosen.astype(jnp.float32), result.astype(jnp.float32)).astype(jnp.bfloat16)
    taken = jnp.any(chosen, axis=2)
    return jnp.where(taken[:, :, None, None], placed, tiles).reshape(PIXELS, SPEC, D)
```

```python
import functools

import jax
import jax.numpy as jnp
from jax import lax
from jax.experimental import pallas as pl
from jax.experimental.pallas import tpu as pltpu
from jax.sharding import PartitionSpec as P

HD = 64
MESH = pl.DeviceIdType.MESH
BF = jnp.bfloat16
F32 = jnp.float32


def normed(full, gain):
    scaled = full * lax.rsqrt(jnp.mean(full * full, axis=-1, keepdims=True) + 1e-05)
    return (scaled * gain).astype(BF)


def kernel(
    nb, np_, spec_here, tile, caps,
    x_ref, count_ref, index_ref, again_ref, mgain_ref,
    wq_h, wk_h, wv_h, wo_h, wg_h, wu_h, wd_h,
    out_ref,
    wq, wk, wv, wo, wg, wu, wd,
    rows_a, marks, qkv, qkv_in, ctx, ctx_in, part1, part1_in, rows_b, part2, part2_in,
    w_sem,
    ag_s, ag_r, mk_s, mk_r, qk_s, qk_r, cx_s, cx_r, p1_s, p1_r, bg_s, bg_r, p2_s, p2_r,
):
    b, t = lax.axis_index("band"), lax.axis_index("pix")
    mine = spec_here * tile
    width = x_ref.shape[1]
    hq = wq.shape[1]
    heads = hq // HD

    loads = []
    for i, (src, dst) in enumerate(
        ((wq_h, wq), (wk_h, wk), (wv_h, wv), (wo_h, wo), (wg_h, wg), (wu_h, wu), (wd_h, wd))
    ):
        load = pltpu.make_async_copy(src, dst, w_sem.at[i])
        load.start()
        loads.append(load)

    band_peers = [(lax.rem(b + k, nb), t) for k in range(1, nb)]
    pix_peers = [(b, lax.rem(t + k, np_)) for k in range(1, np_)]
    barrier = pltpu.get_barrier_semaphore()
    for peer in band_peers + pix_peers:
        pl.semaphore_signal(barrier, inc=1, device_id=peer, device_id_type=MESH)

    def rows_of(ref, i, n):
        return ref.at[pl.ds(pl.multiple_of(i * n, n), n)]

    my_rows = rows_of(rows_a, b, mine)
    my_rows[...] = normed(x_ref[...].astype(F32), again_ref[...])
    spot = lax.broadcasted_iota(jnp.int32, (tile, 128), 0)
    count = count_ref[0]
    live = jnp.zeros((tile, 128), jnp.int32)
    for c in range(caps):
        live = jnp.where((spot == index_ref[c]) & (c < count), 1, live)
    my_mark = rows_of(marks, t, tile)
    my_mark[...] = live.astype(F32).astype(BF)

    pl.semaphore_wait(barrier, len(band_peers) + len(pix_peers))

    def send(src, dst, s_sem, r_sem, k, peer):
        copy = pltpu.make_async_remote_copy(
            src_ref=src, dst_ref=dst, send_sem=s_sem.at[k], recv_sem=r_sem.at[k],
            device_id=peer, device_id_type=MESH,
        )
        copy.start()
        return copy

    gathers = [send(my_rows, my_rows, ag_s, ag_r, k, p) for k, p in enumerate(band_peers)]
    mark_sends = [send(my_mark, my_mark, mk_s, mk_r, k, p) for k, p in enumerate(pix_peers)]

    for load in loads[:3]:
        load.wait()
    for g in gathers:
        g.wait_recv()
    rows = rows_a[...]
    for i, w in enumerate((wq, wk, wv)):
        qkv[:, i * hq : (i + 1) * hq] = jnp.dot(
            rows, w[...], preferred_element_type=F32
        ).astype(BF)

    in_slot = rows_of(qkv_in, t, tile)
    qkv_sends = [
        send(rows_of(qkv, p[1], tile), in_slot, qk_s, qk_r, k, p)
        for k, p in enumerate(pix_peers)
    ]
    in_slot[...] = rows_of(qkv, t, tile)[...]
    for m in mark_sends:
        m.wait_recv()
    lane0 = (lax.broadcasted_iota(jnp.int32, (np_ * tile, 128), 1) == 0).astype(F32).astype(BF)
    alive = (
        lax.dot_general(
            lane0, marks[...], (((1,), (1,)), ((), ())), preferred_element_type=F32
        )
        > 0.5
    )
    for s in qkv_sends:
        s.wait_recv()

    for h in range(heads):
        q = qkv_in[:, h * HD : (h + 1) * HD]
        k = qkv_in[:, hq + h * HD : hq + (h + 1) * HD]
        v = qkv_in[:, 2 * hq + h * HD : 2 * hq + (h + 1) * HD]
        score = lax.dot_general(
            q, k, (((1,), (1,)), ((), ())), preferred_element_type=F32
        ) * HD ** (-0.5)
        masked = jnp.where(alive, score, -1e30)
        top = jnp.max(masked, axis=-1, keepdims=True)
        expo = jnp.where(alive, jnp.exp(masked - top), 0.0)
        total = jnp.sum(expo, axis=-1, keepdims=True)
        mixed = jnp.dot(expo.astype(BF), v, preferred_element_type=F32)
        ctx[:, h * HD : (h + 1) * HD] = (mixed / total).astype(BF)

    ctx_slot = rows_of(ctx_in, t, tile)
    ctx_sends = [
        send(rows_of(ctx, p[1], tile), ctx_slot, cx_s, cx_r, k, p)
        for k, p in enumerate(pix_peers)
    ]
    ctx_slot[...] = rows_of(ctx, t, tile)[...]
    loads[3].wait()
    for s in ctx_sends:
        s.wait_recv()

    def scatter_sum(part, part_in, s_sem, r_sem):
        slot = rows_of(part_in, b, mine)
        sends = [
            send(rows_of(part, p[0], mine), slot, s_sem, r_sem, k, p)
            for k, p in enumerate(band_peers)
        ]
        total = rows_of(part, b, mine)[...].astype(F32)
        for k, s in enumerate(sends):
            s.wait_recv()
            source = lax.rem(b + nb - 1 - k, nb)
            total = total + rows_of(part_in, source, mine)[...].astype(F32)
        return total, sends

    part1[...] = jnp.dot(ctx_in[...], wo[...], preferred_element_type=F32).astype(BF)
    attn_out, sends1 = scatter_sum(part1, part1_in, p1_s, p1_r)
    state = (x_ref[...].astype(F32) + attn_out).astype(BF)

    my_b = rows_of(rows_b, b, mine)
    my_b[...] = normed(state.astype(F32), mgain_ref[...])
    gathers2 = [send(my_b, my_b, bg_s, bg_r, k, p) for k, p in enumerate(band_peers)]
    for load in loads[4:]:
        load.wait()
    for g in gathers2:
        g.wait_recv()
    rows = rows_b[...]
    gate = jnp.dot(rows, wg[...], preferred_element_type=F32)
    upper = jnp.dot(rows, wu[...], preferred_element_type=F32)
    hidden = (gate / (1.0 + jnp.exp(-gate)) * upper).astype(BF)
    part2[...] = jnp.dot(hidden, wd[...], preferred_element_type=F32).astype(BF)
    mlp_out, sends2 = scatter_sum(part2, part2_in, p2_s, p2_r)
    encoded = (state.astype(F32) + mlp_out).astype(BF)
    keep = jnp.concatenate([live[:, :1]] * spec_here, axis=0) > 0
    out_ref[...] = jnp.where(keep, encoded.astype(F32), x_ref[...].astype(F32)).astype(BF)
    for s in gathers + mark_sends + qkv_sends + ctx_sends + sends1 + gathers2 + sends2:
        s.wait_send()


def shards(nb, np_, pixels, clear_count, clear_index, attn_gain, w_query, w_key, w_value, w_out, mlp_gain, w_gate, w_up, w_down):
    tile, spec_here, width = pixels.shape
    spec = spec_here * nb
    mine, rows, slots = spec_here * tile, spec * tile, np_ * tile
    hq = w_query.shape[1]
    weights = (w_query, w_key, w_value, w_out, w_gate, w_up, w_down)
    x = jnp.swapaxes(pixels, 0, 1).reshape(mine, width)
    vmem = pl.BlockSpec(memory_space=pltpu.VMEM)
    smem = pl.BlockSpec(memory_space=pltpu.SMEM)
    dma = pltpu.SemaphoreType.DMA
    out = pl.pallas_call(
        functools.partial(kernel, nb, np_, spec_here, tile, clear_index.shape[0]),
        out_shape=jax.ShapeDtypeStruct((mine, width), BF),
        in_specs=[vmem, smem, smem, vmem, vmem] + [pl.BlockSpec(memory_space=pl.ANY)] * 7,
        out_specs=vmem,
        scratch_shapes=[pltpu.VMEM(w.shape, BF) for w in weights]
        + [
            pltpu.VMEM((rows, width), BF),
            pltpu.VMEM((slots, 128), BF),
            pltpu.VMEM((rows, 3 * hq), BF),
            pltpu.VMEM((slots, 3 * hq), BF),
            pltpu.VMEM((slots, hq), BF),
            pltpu.VMEM((rows, hq), BF),
            pltpu.VMEM((rows, width), BF),
            pltpu.VMEM((rows, width), BF),
            pltpu.VMEM((rows, width), BF),
            pltpu.VMEM((rows, width), BF),
            pltpu.VMEM((rows, width), BF),
            dma((7,)),
        ]
        + [dma((n - 1,)) for n in (nb, np_, np_, np_, nb, nb, nb) for _ in range(2)],
        compiler_params=pltpu.CompilerParams(
            collective_id=0, has_side_effects=True, vmem_limit_bytes=56 * 2**20
        ),
    )(x, clear_count, clear_index, attn_gain.reshape(1, width), mlp_gain.reshape(1, width), *weights)
    return jnp.swapaxes(out.reshape(spec_here, tile, width), 0, 1)


def solution(mesh):
    nb, np_ = mesh.shape["band"], mesh.shape["pix"]
    return jax.shard_map(
        functools.partial(shards, nb, np_),
        mesh=mesh,
        in_specs=(
            P("pix", "band", None),
            P("pix"),
            P("pix"),
            P(),
            P(None, "band"),
            P(None, "band"),
            P(None, "band"),
            P("band", None),
            P(),
            P(None, "band"),
            P(None, "band"),
            P("band", None),
        ),
        out_specs=P("pix", "band", None),
        check_vma=False,
    )
```

```python
import functools

import jax
import jax.numpy as jnp
from jax import lax
from jax.experimental import pallas as pl
from jax.experimental.pallas import tpu as pltpu
from jax.sharding import PartitionSpec as P

HD = 64
MESH = pl.DeviceIdType.MESH
BF = jnp.bfloat16
F32 = jnp.float32


def normed(full, gain):
    scaled = full * lax.rsqrt(jnp.mean(full * full, axis=-1, keepdims=True) + 1e-05)
    return (scaled * gain).astype(BF)


def kernel(
    nb, np_, spec_here, tile, caps,
    pix_h, count_ref, index_ref, again_ref, mgain_ref,
    wq_h, wk_h, wv_h, wo_h, wg_h, wu_h, wd_h,
    out_ref,
    wq, wk, wv, wo, wg, wu, wd,
    pix, x_ref, pix_sem, rows_a, marks, qkv, qkv_in, ctx, ctx_in, part1, part1_in, rows_b, part2, part2_in,
    w_sem,
    ag_s, ag_r, mk_s, mk_r, qk_s, qk_r, cx_s, cx_r, p1_s, p1_r, bg_s, bg_r, p2_s, p2_r,
):
    b, t = lax.axis_index("band"), lax.axis_index("pix")
    mine = spec_here * tile
    hq = wq.shape[1]
    heads = hq // HD

    pix_load = pltpu.make_async_copy(pix_h, pix, pix_sem)
    pix_load.start()
    loads = []
    for i, (src, dst) in enumerate(
        ((wq_h, wq), (wk_h, wk), (wv_h, wv), (wo_h, wo), (wg_h, wg), (wu_h, wu), (wd_h, wd))
    ):
        load = pltpu.make_async_copy(src, dst, w_sem.at[i])
        load.start()
        loads.append(load)

    def others(me, n):
        if n & (n - 1) == 0:
            return [jnp.bitwise_xor(me, k) for k in range(n - 1, 0, -1)]
        return [lax.rem(me + k, n) for k in range(1, n)]

    def source(me, n, k, peer):
        return peer if n & (n - 1) == 0 else lax.rem(me + n - 1 - k, n)

    band_peers = [(p, t) for p in others(b, nb)]
    pix_peers = [(b, p) for p in others(t, np_)]
    barrier = pltpu.get_barrier_semaphore()
    for peer in pix_peers + band_peers:
        pl.semaphore_signal(barrier, inc=1, device_id=peer, device_id_type=MESH)

    def rows_of(ref, i, n):
        return ref.at[pl.ds(pl.multiple_of(i * n, n), n)]

    my_rows = rows_of(rows_a, b, mine)
    pix_load.wait()
    raw = pix[...].astype(F32)
    for s in range(spec_here):
        x_ref[s * tile : (s + 1) * tile, :] = raw[:, s, :]
    my_rows[...] = normed(x_ref[...], again_ref[...])
    spot = lax.broadcasted_iota(jnp.int32, (tile, 128), 0)
    count = count_ref[0]
    live = jnp.zeros((tile, 128), jnp.int32)
    for c in range(caps):
        live = jnp.where((spot == index_ref[c]) & (c < count), 1, live)
    my_mark = rows_of(marks, t, tile)
    my_mark[...] = live.astype(F32).astype(BF)

    pl.semaphore_wait(barrier, len(band_peers) + len(pix_peers))

    def send(src, dst, s_sem, r_sem, k, peer):
        copy = pltpu.make_async_remote_copy(
            src_ref=src, dst_ref=dst, send_sem=s_sem.at[k], recv_sem=r_sem.at[k],
            device_id=peer, device_id_type=MESH,
        )
        copy.start()
        return copy

    gathers = [send(my_rows, my_rows, ag_s, ag_r, k, p) for k, p in enumerate(band_peers)]
    mark_sends = [send(my_mark, my_mark, mk_s, mk_r, k, p) for k, p in enumerate(pix_peers)]

    for load in loads[:3]:
        load.wait()
    for g in gathers:
        g.wait_recv()
    rows = rows_a[...]
    for i, w in enumerate((wq, wk, wv)):
        qkv[:, i * hq : (i + 1) * hq] = jnp.dot(
            rows, w[...], preferred_element_type=F32
        ).astype(BF)

    in_slot = rows_of(qkv_in, t, tile)
    qkv_sends = [
        send(rows_of(qkv, p[1], tile), in_slot, qk_s, qk_r, k, p)
        for k, p in enumerate(pix_peers)
    ]
    in_slot[...] = rows_of(qkv, t, tile)[...]
    for m in mark_sends:
        m.wait_recv()
    lane0 = (lax.broadcasted_iota(jnp.int32, (np_ * tile, 128), 1) == 0).astype(F32).astype(BF)
    alive = (
        lax.dot_general(
            lane0, marks[...], (((1,), (1,)), ((), ())), preferred_element_type=F32
        )
        > 0.5
    )
    for s in qkv_sends:
        s.wait_recv()

    for h in range(heads):
        q = qkv_in[:, h * HD : (h + 1) * HD]
        k = qkv_in[:, hq + h * HD : hq + (h + 1) * HD]
        v = qkv_in[:, 2 * hq + h * HD : 2 * hq + (h + 1) * HD]
        score = lax.dot_general(
            q, k, (((1,), (1,)), ((), ())), preferred_element_type=F32
        ) * HD ** (-0.5)
        masked = jnp.where(alive, score, -1e30)
        top = jnp.max(masked, axis=-1, keepdims=True)
        expo = jnp.where(alive, jnp.exp(masked - top), 0.0)
        total = jnp.sum(expo, axis=-1, keepdims=True)
        mixed = jnp.dot(expo.astype(BF), v, preferred_element_type=F32)
        ctx[:, h * HD : (h + 1) * HD] = (mixed / total).astype(BF)

    ctx_slot = rows_of(ctx_in, t, tile)
    ctx_sends = [
        send(rows_of(ctx, p[1], tile), ctx_slot, cx_s, cx_r, k, p)
        for k, p in enumerate(pix_peers)
    ]
    ctx_slot[...] = rows_of(ctx, t, tile)[...]
    loads[3].wait()
    for s in ctx_sends:
        s.wait_recv()

    def scatter_sum(part, part_in, s_sem, r_sem):
        slot = rows_of(part_in, b, mine)
        sends = [
            send(rows_of(part, p[0], mine), slot, s_sem, r_sem, k, p)
            for k, p in enumerate(band_peers)
        ]
        total = rows_of(part, b, mine)[...].astype(F32)
        for k, s in enumerate(sends):
            s.wait_recv()
            sender = source(b, nb, k, band_peers[k][0])
            total = total + rows_of(part_in, sender, mine)[...].astype(F32)
        return total, sends

    part1[...] = jnp.dot(ctx_in[...], wo[...], preferred_element_type=F32).astype(BF)
    attn_out, sends1 = scatter_sum(part1, part1_in, p1_s, p1_r)
    state = (x_ref[...] + attn_out).astype(BF)

    my_b = rows_of(rows_b, b, mine)
    my_b[...] = normed(state.astype(F32), mgain_ref[...])
    gathers2 = [send(my_b, my_b, bg_s, bg_r, k, p) for k, p in enumerate(band_peers)]
    for load in loads[4:]:
        load.wait()
    for g in gathers2:
        g.wait_recv()
    rows = rows_b[...]
    gate = jnp.dot(rows, wg[...], preferred_element_type=F32)
    upper = jnp.dot(rows, wu[...], preferred_element_type=F32)
    hidden = (gate / (1.0 + jnp.exp(-gate)) * upper).astype(BF)
    part2[...] = jnp.dot(hidden, wd[...], preferred_element_type=F32).astype(BF)
    mlp_out, sends2 = scatter_sum(part2, part2_in, p2_s, p2_r)
    encoded = (state.astype(F32) + mlp_out).astype(BF)
    keep = jnp.concatenate([live[:, :1]] * spec_here, axis=0) > 0
    out_ref[...] = jnp.where(keep, encoded.astype(F32), x_ref[...]).astype(BF)
    for s in gathers + mark_sends + qkv_sends + ctx_sends + sends1 + gathers2 + sends2:
        s.wait_send()


def shards(nb, np_, pixels, clear_count, clear_index, attn_gain, w_query, w_key, w_value, w_out, mlp_gain, w_gate, w_up, w_down):
    tile, spec_here, width = pixels.shape
    spec = spec_here * nb
    mine, rows, slots = spec_here * tile, spec * tile, np_ * tile
    hq = w_query.shape[1]
    weights = (w_query, w_key, w_value, w_out, w_gate, w_up, w_down)
    vmem = pl.BlockSpec(memory_space=pltpu.VMEM)
    smem = pl.BlockSpec(memory_space=pltpu.SMEM)
    dma = pltpu.SemaphoreType.DMA
    out = pl.pallas_call(
        functools.partial(kernel, nb, np_, spec_here, tile, clear_index.shape[0]),
        out_shape=jax.ShapeDtypeStruct((mine, width), BF),
        in_specs=[pl.BlockSpec(memory_space=pl.ANY), smem, smem, vmem, vmem] + [pl.BlockSpec(memory_space=pl.ANY)] * 7,
        out_specs=vmem,
        scratch_shapes=[pltpu.VMEM(w.shape, BF) for w in weights]
        + [
            pltpu.VMEM(pixels.shape, BF),
            pltpu.VMEM((mine, width), F32),
            dma(()),
            pltpu.VMEM((rows, width), BF),
            pltpu.VMEM((slots, 128), BF),
            pltpu.VMEM((rows, 3 * hq), BF),
            pltpu.VMEM((slots, 3 * hq), BF),
            pltpu.VMEM((slots, hq), BF),
            pltpu.VMEM((rows, hq), BF),
            pltpu.VMEM((rows, width), BF),
            pltpu.VMEM((rows, width), BF),
            pltpu.VMEM((rows, width), BF),
            pltpu.VMEM((rows, width), BF),
            pltpu.VMEM((rows, width), BF),
            dma((7,)),
        ]
        + [dma((n - 1,)) for n in (nb, np_, np_, np_, nb, nb, nb) for _ in range(2)],
        compiler_params=pltpu.CompilerParams(
            collective_id=0, has_side_effects=True, vmem_limit_bytes=56 * 2**20
        ),
    )(pixels, clear_count, clear_index, attn_gain.reshape(1, width), mlp_gain.reshape(1, width), *weights)
    return jnp.swapaxes(out.reshape(spec_here, tile, width), 0, 1)


def solution(mesh):
    nb, np_ = mesh.shape["band"], mesh.shape["pix"]
    return jax.shard_map(
        functools.partial(shards, nb, np_),
        mesh=mesh,
        in_specs=(
            P("pix", "band", None),
            P("pix"),
            P("pix"),
            P(),
            P(None, "band"),
            P(None, "band"),
            P(None, "band"),
            P("band", None),
            P(),
            P(None, "band"),
            P(None, "band"),
            P("band", None),
        ),
        out_specs=P("pix", "band", None),
        check_vma=False,
    )
```

```python
import functools

import jax
import jax.numpy as jnp
from jax import lax
from jax.experimental import pallas as pl
from jax.experimental.pallas import tpu as pltpu
from jax.sharding import PartitionSpec as P

HD = 64
MESH = pl.DeviceIdType.MESH
BF = jnp.bfloat16
F32 = jnp.float32


def normed(full, gain):
    scaled = full * lax.rsqrt(jnp.mean(full * full, axis=-1, keepdims=True) + 1e-05)
    return (scaled * gain).astype(BF)


def kernel(
    nb, np_, spec_here, tile, caps,
    pix_h, count_ref, index_ref, again_ref, mgain_ref,
    wq_h, wk_h, wv_h, wo_h, wg_h, wu_h, wd_h,
    out_ref,
    wq, wk, wv, wo, wg, wu, wd,
    pix, x_ref, pix_sem, rows_a, marks, qkv, qkv_in, ctx, ctx_in, part1, part1_in, rows_b, part2, part2_in,
    w_sem,
    ag_s, ag_r, mk_s, mk_r, qk_s, qk_r, cx_s, cx_r, p1_s, p1_r, bg_s, bg_r, p2_s, p2_r,
):
    b, t = lax.axis_index("band"), lax.axis_index("pix")
    hq = wq.shape[1]
    heads = hq // HD

    pix_load = pltpu.make_async_copy(pix_h, pix, pix_sem)
    pix_load.start()
    loads = []
    for i, (src, dst) in enumerate(
        ((wq_h, wq), (wk_h, wk), (wv_h, wv), (wo_h, wo), (wg_h, wg), (wu_h, wu), (wd_h, wd))
    ):
        load = pltpu.make_async_copy(src, dst, w_sem.at[i])
        load.start()
        loads.append(load)

    def others(me, n):
        if n & (n - 1) == 0:
            return [jnp.bitwise_xor(me, k) for k in range(n - 1, 0, -1)]
        return [lax.rem(me + k, n) for k in range(1, n)]

    def source(me, n, k, peer):
        return peer if n & (n - 1) == 0 else lax.rem(me + n - 1 - k, n)

    band_peers = [(p, t) for p in others(b, nb)]
    pix_peers = [(b, p) for p in others(t, np_)]
    barrier = pltpu.get_barrier_semaphore()
    for peer in pix_peers + band_peers:
        pl.semaphore_signal(barrier, inc=1, device_id=peer, device_id_type=MESH)

    def rows_of(ref, i, n):
        return ref.at[pl.ds(pl.multiple_of(i * n, n), n)]

    halves = range(spec_here)
    span = nb * tile
    z, core = t // spec_here, lax.rem(t, spec_here)
    pix_load.wait()
    raw = pix[...].astype(F32)
    for h in halves:
        x_ref[h * tile : (h + 1) * tile, :] = raw[:, h, :]
        rows_of(rows_a, h * nb + b, tile)[...] = normed(raw[:, h, :], again_ref[...])
    spot = lax.broadcasted_iota(jnp.int32, (tile, 128), 0)
    count = count_ref[0]
    live = jnp.zeros((tile, 128), jnp.int32)
    for c in range(caps):
        live = jnp.where((spot == index_ref[c]) & (c < count), 1, live)
    my_mark = rows_of(marks, t, tile)
    my_mark[...] = live.astype(F32).astype(BF)

    pl.semaphore_wait(barrier, len(band_peers) + len(pix_peers))

    def link(src, dst, s_sem, r_sem, peer):
        return pltpu.make_async_remote_copy(
            src_ref=src, dst_ref=dst, send_sem=s_sem, recv_sem=r_sem,
            device_id=peer, device_id_type=MESH,
        )

    def send(src, dst, s_sem, r_sem, k, peer):
        copy = link(src, dst, s_sem.at[k], r_sem.at[k], peer)
        copy.start()
        return copy

    def gather_half(ref, h, s_sem, r_sem):
        block = rows_of(ref, h * nb + b, tile)
        return [
            send(block, block, s_sem, r_sem, h * (nb - 1) + k, p)
            for k, p in enumerate(band_peers)
        ]

    def scatter_half(part, part_in, h, s_sem, r_sem):
        slot = rows_of(part_in, h * nb + b, tile)
        return [
            send(rows_of(part, h * nb + p[0], tile), slot, s_sem, r_sem, h * (nb - 1) + k, p)
            for k, p in enumerate(band_peers)
        ]

    def sum_half(part, part_in, h, sends):
        total = rows_of(part, h * nb + b, tile)[...].astype(F32)
        for k, s in enumerate(sends):
            s.wait_recv()
            sender = source(b, nb, k, band_peers[k][0])
            total = total + rows_of(part_in, h * nb + sender, tile)[...].astype(F32)
        return total

    far = range(nb - 1, -1, -1)

    def partner(i, c):
        return jnp.bitwise_xor(z, i)

    def unless_own(i, c, act):
        if i == 0:
            pl.when(core != c)(act)
        else:
            act()

    def pix_copies(src, dst_of, s_sem, r_sem, c):
        made = []
        for i in far:
            to = partner(i, c)
            copy = link(
                src(to, c), dst_of, s_sem.at[c * nb + i], r_sem.at[core * nb + i],
                (b, to * spec_here + c),
            )
            unless_own(i, c, copy.start)
            made.append((i, c, copy))

        @pl.when(core == c)
        def _():
            dst_of[...] = src(z, c)[...]

        return made

    def pix_wait(ref, s_sem, r_sem, c):
        block = rows_of(ref, 0, tile)
        for i in far:
            copy = link(
                block, block, s_sem.at[c * nb + i], r_sem.at[c * nb + i],
                (b, partner(i, c) * spec_here + c),
            )
            unless_own(i, c, copy.wait_recv)

    sent = []
    pix_sent = []
    gathers = [gather_half(rows_a, h, ag_s, ag_r) for h in halves]
    mark_sends = [send(my_mark, my_mark, mk_s, mk_r, k, p) for k, p in enumerate(pix_peers)]
    for load in loads[:3]:
        load.wait()
    for h in halves:
        for g in gathers[h]:
            g.wait_recv()
        rows = rows_a[h * span : (h + 1) * span, :]
        for i, w in enumerate((wq, wk, wv)):
            qkv[h * span : (h + 1) * span, i * hq : (i + 1) * hq] = jnp.dot(
                rows, w[...], preferred_element_type=F32
            ).astype(BF)
        pix_sent += pix_copies(
            lambda to, c: rows_of(qkv, c * nb + to, tile),
            rows_of(qkv_in, t, tile), qk_s, qk_r, h,
        )
    for m in mark_sends:
        m.wait_recv()
    lane0 = (lax.broadcasted_iota(jnp.int32, (np_ * tile, 128), 1) == 0).astype(F32).astype(BF)
    alive = (
        lax.dot_general(
            lane0, marks[...], (((1,), (1,)), ((), ())), preferred_element_type=F32
        )
        > 0.5
    )
    for c in halves:
        pix_wait(qkv_in, qk_s, qk_r, c)

    for h in range(heads):
        q = qkv_in[:, h * HD : (h + 1) * HD]
        k = qkv_in[:, hq + h * HD : hq + (h + 1) * HD]
        v = qkv_in[:, 2 * hq + h * HD : 2 * hq + (h + 1) * HD]
        score = lax.dot_general(
            q, k, (((1,), (1,)), ((), ())), preferred_element_type=F32
        ) * HD ** (-0.5)
        masked = jnp.where(alive, score, -1e30)
        top = jnp.max(masked, axis=-1, keepdims=True)
        expo = jnp.where(alive, jnp.exp(masked - top), 0.0)
        total = jnp.sum(expo, axis=-1, keepdims=True)
        mixed = jnp.dot(expo.astype(BF), v, preferred_element_type=F32)
        ctx[:, h * HD : (h + 1) * HD] = (mixed / total).astype(BF)

    for c in halves:
        pix_sent += pix_copies(
            lambda to, c: rows_of(ctx, to * spec_here + c, tile),
            rows_of(ctx_in, core * nb + z, tile), cx_s, cx_r, c,
        )
    loads[3].wait()
    sums = []
    for h in halves:
        pix_wait(ctx_in, cx_s, cx_r, h)
        part1[h * span : (h + 1) * span, :] = jnp.dot(
            ctx_in[h * span : (h + 1) * span, :], wo[...], preferred_element_type=F32
        ).astype(BF)
        sums.append(scatter_half(part1, part1_in, h, p1_s, p1_r))
    sent += sums
    states, gathers2 = [], []
    for h in halves:
        attn_out = sum_half(part1, part1_in, h, sums[h])
        state = (x_ref[h * tile : (h + 1) * tile, :] + attn_out).astype(BF).astype(F32)
        states.append(state)
        rows_of(rows_b, h * nb + b, tile)[...] = normed(state, mgain_ref[...])
        gathers2.append(gather_half(rows_b, h, bg_s, bg_r))
    for load in loads[4:]:
        load.wait()
    sums2 = []
    for h in halves:
        for g in gathers2[h]:
            g.wait_recv()
        rows = rows_b[h * span : (h + 1) * span, :]
        gate = jnp.dot(rows, wg[...], preferred_element_type=F32)
        upper = jnp.dot(rows, wu[...], preferred_element_type=F32)
        hidden = (gate / (1.0 + jnp.exp(-gate)) * upper).astype(BF)
        part2[h * span : (h + 1) * span, :] = jnp.dot(
            hidden, wd[...], preferred_element_type=F32
        ).astype(BF)
        sums2.append(scatter_half(part2, part2_in, h, p2_s, p2_r))
    for h in halves:
        encoded = (states[h] + sum_half(part2, part2_in, h, sums2[h])).astype(BF)
        own = slice(h * tile, (h + 1) * tile)
        out_ref[own, :] = jnp.where(
            live[:, :1] > 0, encoded.astype(F32), x_ref[own, :]
        ).astype(BF)
    for group in gathers + [mark_sends] + sent + gathers2 + sums2:
        for s in group:
            s.wait_send()
    for i, c, copy in pix_sent:
        unless_own(i, c, copy.wait_send)


def shards(nb, np_, pixels, clear_count, clear_index, attn_gain, w_query, w_key, w_value, w_out, mlp_gain, w_gate, w_up, w_down):
    tile, spec_here, width = pixels.shape
    spec = spec_here * nb
    pairs = spec_here * (nb - 1)
    assert spec == np_ and nb & (nb - 1) == 0
    mine, rows, slots = spec_here * tile, spec * tile, np_ * tile
    hq = w_query.shape[1]
    weights = (w_query, w_key, w_value, w_out, w_gate, w_up, w_down)
    vmem = pl.BlockSpec(memory_space=pltpu.VMEM)
    smem = pl.BlockSpec(memory_space=pltpu.SMEM)
    dma = pltpu.SemaphoreType.DMA
    out = pl.pallas_call(
        functools.partial(kernel, nb, np_, spec_here, tile, clear_index.shape[0]),
        out_shape=jax.ShapeDtypeStruct((mine, width), BF),
        in_specs=[pl.BlockSpec(memory_space=pl.ANY), smem, smem, vmem, vmem] + [pl.BlockSpec(memory_space=pl.ANY)] * 7,
        out_specs=vmem,
        scratch_shapes=[pltpu.VMEM(w.shape, BF) for w in weights]
        + [
            pltpu.VMEM(pixels.shape, BF),
            pltpu.VMEM((mine, width), F32),
            dma(()),
            pltpu.VMEM((rows, width), BF),
            pltpu.VMEM((slots, 128), BF),
            pltpu.VMEM((rows, 3 * hq), BF),
            pltpu.VMEM((slots, 3 * hq), BF),
            pltpu.VMEM((slots, hq), BF),
            pltpu.VMEM((rows, hq), BF),
            pltpu.VMEM((rows, width), BF),
            pltpu.VMEM((rows, width), BF),
            pltpu.VMEM((rows, width), BF),
            pltpu.VMEM((rows, width), BF),
            pltpu.VMEM((rows, width), BF),
            dma((7,)),
        ]
        + [dma((n,)) for n in (pairs, np_ - 1, np_, np_, pairs, pairs, pairs) for _ in range(2)],
        compiler_params=pltpu.CompilerParams(
            collective_id=0, has_side_effects=True, vmem_limit_bytes=56 * 2**20
        ),
    )(pixels, clear_count, clear_index, attn_gain.reshape(1, width), mlp_gain.reshape(1, width), *weights)
    return jnp.swapaxes(out.reshape(spec_here, tile, width), 0, 1)


def solution(mesh):
    nb, np_ = mesh.shape["band"], mesh.shape["pix"]
    return jax.shard_map(
        functools.partial(shards, nb, np_),
        mesh=mesh,
        in_specs=(
            P("pix", "band", None),
            P("pix"),
            P("pix"),
            P(),
            P(None, "band"),
            P(None, "band"),
            P(None, "band"),
            P("band", None),
            P(),
            P(None, "band"),
            P(None, "band"),
            P("band", None),
        ),
        out_specs=P("pix", "band", None),
        check_vma=False,
    )
```

```python
import functools

import jax
import jax.numpy as jnp
from jax import lax
from jax.experimental import pallas as pl
from jax.experimental.pallas import tpu as pltpu
from jax.sharding import PartitionSpec as P

HD = 64
MESH = pl.DeviceIdType.MESH
BF = jnp.bfloat16
F32 = jnp.float32


def normed(full, gain):
    scaled = full * lax.rsqrt(jnp.mean(full * full, axis=-1, keepdims=True) + 1e-05)
    return (scaled * gain).astype(BF)


def kernel(
    nb, np_, spec_here, tile, caps,
    pix_h, count_ref, index_ref, again_ref, mgain_ref,
    wq_h, wk_h, wv_h, wo_h, wg_h, wu_h, wd_h,
    out_ref,
    wq, wk, wv, wo, wg, wu, wd,
    pix, x_ref, pix_sem, rows_a, marks, qkv, qkv_in, ctx, ctx_in, part1, part1_in, rows_b, part2, part2_in,
    w_sem,
    ag_s, ag_r, mk_s, mk_r, qk_s, qk_r, cx_s, cx_r, p1_s, p1_r, bg_s, bg_r, p2_s, p2_r,
):
    b, t = lax.axis_index("band"), lax.axis_index("pix")
    hq = wq.shape[1]
    heads = hq // HD

    pix_load = pltpu.make_async_copy(pix_h, pix, pix_sem)
    pix_load.start()
    def others(me, n):
        if n & (n - 1) == 0:
            return [jnp.bitwise_xor(me, k) for k in range(n - 1, 0, -1)]
        return [lax.rem(me + k, n) for k in range(1, n)]

    def source(me, n, k, peer):
        return peer if n & (n - 1) == 0 else lax.rem(me + n - 1 - k, n)

    band_peers = [(p, t) for p in others(b, nb)]
    pix_peers = [(b, p) for p in others(t, np_)]
    barrier = pltpu.get_barrier_semaphore()
    for peer in pix_peers + band_peers:
        pl.semaphore_signal(barrier, inc=1, device_id=peer, device_id_type=MESH)

    loads = []
    for i, (src, dst) in enumerate(
        ((wq_h, wq), (wk_h, wk), (wv_h, wv), (wo_h, wo), (wg_h, wg), (wu_h, wu), (wd_h, wd))
    ):
        load = pltpu.make_async_copy(src, dst, w_sem.at[i])
        load.start()
        loads.append(load)

    def rows_of(ref, i, n):
        return ref.at[pl.ds(pl.multiple_of(i * n, n), n)]

    halves = range(spec_here)
    span = nb * tile
    z, core = t // spec_here, lax.rem(t, spec_here)
    pix_load.wait()
    raw = pix[...].astype(F32)
    for h in halves:
        x_ref[h * tile : (h + 1) * tile, :] = raw[:, h, :]
        rows_of(rows_a, h * nb + b, tile)[...] = normed(raw[:, h, :], again_ref[...])
    spot = lax.broadcasted_iota(jnp.int32, (tile, 128), 0)
    count = count_ref[0]
    live = jnp.zeros((tile, 128), jnp.int32)
    for c in range(caps):
        live = jnp.where((spot == index_ref[c]) & (c < count), 1, live)
    my_mark = rows_of(marks, t, tile)
    my_mark[...] = live.astype(F32).astype(BF)

    pl.semaphore_wait(barrier, len(band_peers) + len(pix_peers))

    def link(src, dst, s_sem, r_sem, peer):
        return pltpu.make_async_remote_copy(
            src_ref=src, dst_ref=dst, send_sem=s_sem, recv_sem=r_sem,
            device_id=peer, device_id_type=MESH,
        )

    def send(src, dst, s_sem, r_sem, k, peer):
        copy = link(src, dst, s_sem.at[k], r_sem.at[k], peer)
        copy.start()
        return copy

    def gather_half(ref, h, s_sem, r_sem):
        block = rows_of(ref, h * nb + b, tile)
        return [
            send(block, block, s_sem, r_sem, h * (nb - 1) + k, p)
            for k, p in enumerate(band_peers)
        ]

    def scatter_half(part, part_in, h, s_sem, r_sem):
        slot = rows_of(part_in, h * nb + b, tile)
        return [
            send(rows_of(part, h * nb + p[0], tile), slot, s_sem, r_sem, h * (nb - 1) + k, p)
            for k, p in enumerate(band_peers)
        ]

    def sum_half(part, part_in, h, sends):
        total = rows_of(part, h * nb + b, tile)[...].astype(F32)
        for k, s in enumerate(sends):
            s.wait_recv()
            sender = source(b, nb, k, band_peers[k][0])
            total = total + rows_of(part_in, h * nb + sender, tile)[...].astype(F32)
        return total

    far = range(nb - 1, -1, -1)

    def partner(i, c):
        return jnp.bitwise_xor(z, i)

    def unless_own(i, c, act):
        if i == 0:
            pl.when(core != c)(act)
        else:
            act()

    def pix_copies(src, dst_of, s_sem, r_sem, c):
        made = []
        for i in far:
            to = partner(i, c)
            copy = link(
                src(to, c), dst_of, s_sem.at[c * nb + i], r_sem.at[core * nb + i],
                (b, to * spec_here + c),
            )
            unless_own(i, c, copy.start)
            made.append((i, c, copy))

        @pl.when(core == c)
        def _():
            dst_of[...] = src(z, c)[...]

        return made

    def pix_wait(ref, s_sem, r_sem, c):
        block = rows_of(ref, 0, tile)
        for i in far:
            copy = link(
                block, block, s_sem.at[c * nb + i], r_sem.at[c * nb + i],
                (b, partner(i, c) * spec_here + c),
            )
            unless_own(i, c, copy.wait_recv)

    sent = []
    pix_sent = []
    gathers = [gather_half(rows_a, h, ag_s, ag_r) for h in halves]
    mark_sends = [send(my_mark, my_mark, mk_s, mk_r, k, p) for k, p in enumerate(pix_peers)]
    for load in loads[:3]:
        load.wait()
    for h in halves:
        for g in gathers[h]:
            g.wait_recv()
        rows = rows_a[h * span : (h + 1) * span, :]
        for i, w in enumerate((wq, wk, wv)):
            qkv[h * span : (h + 1) * span, i * hq : (i + 1) * hq] = jnp.dot(
                rows, w[...], preferred_element_type=F32
            ).astype(BF)
        pix_sent += pix_copies(
            lambda to, c: rows_of(qkv, c * nb + to, tile),
            rows_of(qkv_in, t, tile), qk_s, qk_r, h,
        )
    for m in mark_sends:
        m.wait_recv()
    lane0 = (lax.broadcasted_iota(jnp.int32, (np_ * tile, 128), 1) == 0).astype(F32).astype(BF)
    alive = (
        lax.dot_general(
            lane0, marks[...], (((1,), (1,)), ((), ())), preferred_element_type=F32
        )
        > 0.5
    )
    for c in halves:
        pix_wait(qkv_in, qk_s, qk_r, c)

    for h in range(heads):
        q = qkv_in[:, h * HD : (h + 1) * HD]
        k = qkv_in[:, hq + h * HD : hq + (h + 1) * HD]
        v = qkv_in[:, 2 * hq + h * HD : 2 * hq + (h + 1) * HD]
        score = lax.dot_general(
            q, k, (((1,), (1,)), ((), ())), preferred_element_type=F32
        ) * HD ** (-0.5)
        masked = jnp.where(alive, score, -1e30)
        top = jnp.max(masked, axis=-1, keepdims=True)
        expo = jnp.where(alive, jnp.exp(masked - top), 0.0)
        total = jnp.sum(expo, axis=-1, keepdims=True)
        mixed = jnp.dot(expo.astype(BF), v, preferred_element_type=F32)
        ctx[:, h * HD : (h + 1) * HD] = (mixed / total).astype(BF)

    for c in halves:
        pix_sent += pix_copies(
            lambda to, c: rows_of(ctx, to * spec_here + c, tile),
            rows_of(ctx_in, core * nb + z, tile), cx_s, cx_r, c,
        )
    loads[3].wait()
    sums = []
    for h in halves:
        pix_wait(ctx_in, cx_s, cx_r, h)
        part1[h * span : (h + 1) * span, :] = jnp.dot(
            ctx_in[h * span : (h + 1) * span, :], wo[...], preferred_element_type=F32
        ).astype(BF)
        sums.append(scatter_half(part1, part1_in, h, p1_s, p1_r))
    sent += sums
    states, gathers2 = [], []
    for h in halves:
        attn_out = sum_half(part1, part1_in, h, sums[h])
        state = (x_ref[h * tile : (h + 1) * tile, :] + attn_out).astype(BF).astype(F32)
        states.append(state)
        rows_of(rows_b, h * nb + b, tile)[...] = normed(state, mgain_ref[...])
        gathers2.append(gather_half(rows_b, h, bg_s, bg_r))
    for load in loads[4:]:
        load.wait()
    sums2 = []
    for h in halves:
        for g in gathers2[h]:
            g.wait_recv()
        rows = rows_b[h * span : (h + 1) * span, :]
        gate = jnp.dot(rows, wg[...], preferred_element_type=F32)
        upper = jnp.dot(rows, wu[...], preferred_element_type=F32)
        hidden = (gate / (1.0 + jnp.exp(-gate)) * upper).astype(BF)
        part2[h * span : (h + 1) * span, :] = jnp.dot(
            hidden, wd[...], preferred_element_type=F32
        ).astype(BF)
        sums2.append(scatter_half(part2, part2_in, h, p2_s, p2_r))
    for h in halves:
        encoded = (states[h] + sum_half(part2, part2_in, h, sums2[h])).astype(BF)
        own = slice(h * tile, (h + 1) * tile)
        out_ref[own, :] = jnp.where(
            live[:, :1] > 0, encoded.astype(F32), x_ref[own, :]
        ).astype(BF)
    for group in gathers + [mark_sends] + sent + gathers2 + sums2:
        for s in group:
            s.wait_send()
    for i, c, copy in pix_sent:
        unless_own(i, c, copy.wait_send)


def shards(nb, np_, pixels, clear_count, clear_index, attn_gain, w_query, w_key, w_value, w_out, mlp_gain, w_gate, w_up, w_down):
    tile, spec_here, width = pixels.shape
    spec = spec_here * nb
    pairs = spec_here * (nb - 1)
    assert spec == np_ and nb & (nb - 1) == 0
    mine, rows, slots = spec_here * tile, spec * tile, np_ * tile
    hq = w_query.shape[1]
    weights = (w_query, w_key, w_value, w_out, w_gate, w_up, w_down)
    vmem = pl.BlockSpec(memory_space=pltpu.VMEM)
    smem = pl.BlockSpec(memory_space=pltpu.SMEM)
    dma = pltpu.SemaphoreType.DMA
    out = pl.pallas_call(
        functools.partial(kernel, nb, np_, spec_here, tile, clear_index.shape[0]),
        out_shape=jax.ShapeDtypeStruct((mine, width), BF),
        in_specs=[pl.BlockSpec(memory_space=pl.ANY), smem, smem, vmem, vmem] + [pl.BlockSpec(memory_space=pl.ANY)] * 7,
        out_specs=vmem,
        scratch_shapes=[pltpu.VMEM(w.shape, BF) for w in weights]
        + [
            pltpu.VMEM(pixels.shape, BF),
            pltpu.VMEM((mine, width), F32),
            dma(()),
            pltpu.VMEM((rows, width), BF),
            pltpu.VMEM((slots, 128), BF),
            pltpu.VMEM((rows, 3 * hq), BF),
            pltpu.VMEM((slots, 3 * hq), BF),
            pltpu.VMEM((slots, hq), BF),
            pltpu.VMEM((rows, hq), BF),
            pltpu.VMEM((rows, width), BF),
            pltpu.VMEM((rows, width), BF),
            pltpu.VMEM((rows, width), BF),
            pltpu.VMEM((rows, width), BF),
            pltpu.VMEM((rows, width), BF),
            dma((7,)),
        ]
        + [dma((n,)) for n in (pairs, np_ - 1, np_, np_, pairs, pairs, pairs) for _ in range(2)],
        compiler_params=pltpu.CompilerParams(
            collective_id=0, has_side_effects=True, vmem_limit_bytes=56 * 2**20
        ),
    )(pixels, clear_count, clear_index, attn_gain.reshape(1, width), mlp_gain.reshape(1, width), *weights)
    return jnp.swapaxes(out.reshape(spec_here, tile, width), 0, 1)


def solution(mesh):
    nb, np_ = mesh.shape["band"], mesh.shape["pix"]
    return jax.shard_map(
        functools.partial(shards, nb, np_),
        mesh=mesh,
        in_specs=(
            P("pix", "band", None),
            P("pix"),
            P("pix"),
            P(),
            P(None, "band"),
            P(None, "band"),
            P(None, "band"),
            P("band", None),
            P(),
            P(None, "band"),
            P(None, "band"),
            P("band", None),
        ),
        out_specs=P("pix", "band", None),
        check_vma=False,
    )
```
